32 devices in a mesh: groups: 2 (over x), tensor: 8 (over z, y), section: 2 (over core).
Axes of the slice: x: 2, y: 2, z: 4, core: 2. Of those that a mesh axis runs over, the one named last changes fastest.
Arguments:
- hidden: bfloat16 [2, 768, 32768], P('section', 'groups', 'tensor'), parts along dimension 1, may hold values from -6 to 6
- down_weight: bfloat16 [2, 32768, 8192], P('section', 'tensor'), may hold values from -0.046875 to 0.046875
- stream: bfloat16 [2, 768, 8192], P('section', 'groups', 'tensor'), parts along dimension 1, may hold values from -36 to 36
- norm_gain: bfloat16 [2, 8192], P('section', 'tensor'), may hold values from 0.25 to 1.75
Outputs:
- new_stream: bfloat16 [2, 768, 8192], P('section', 'groups', 'tensor'), parts along dimension 1
- next_input: bfloat16 [2, 768, 8192], P('section', 'groups', 'tensor'), parts along dimension 1
The draws below stay inside these ranges and needn't reach their ends.
There are 2 independent parts, one for each index of `groups`. The reference program is written for one: setup_inputs(seed, part) draws one part's arguments, and reference() takes and returns one part's arrays. A program takes and returns all parts, laid end to end along the dimension named above; an argument that names none is the same for every part. Nothing has to cross between parts.
All inputs are finite; a program needn't handle non-finite values.
Results may differ from the reference program's by a relative error of at most 0.0015.
Values may be sent and summed in bfloat16 or wider, within the bound.
No kernel may reach another device: no remote copies, remote signals or barrier semaphores. Data moves between devices by JAX's collectives and lax.ppermute only.
A program may use at most 192 MiB of HBM per device.

```python
import jax
import jax.numpy as jnp
from jax import lax

D = 8192
FF = 32768
ROWS = 384
SECTIONS = 2


def draw_stream(key, part):
    key = jax.random.fold_in(key, 7)
    first_key, second_key = jax.random.split(key, 2)
    column = jnp.arange(D, dtype=jnp.float32) / D
    row_scale = jnp.exp(jax.random.uniform(second_key, (SECTIONS, ROWS, 1), jnp.float32, -0.8, 0.8))
    base = jax.random.truncated_normal(first_key, -4.0, 4.0, (SECTIONS, ROWS, D), jnp.float32)
    values = base * row_scale * (0.4 * 10.0 ** column)
    return values.astype(jnp.bfloat16)


def spiked(array, stream_key, source, target, blocks, factor):
    def block_of(axis_at):
        return (jnp.arange(array.shape[axis_at]) // (array.shape[axis_at] // blocks)).reshape((-1,) + (1,) * (array.ndim - 1 - axis_at))

    one_side = jax.random.permutation(stream_key, blocks)[block_of(target)]
    far = (block_of(target) + blocks // 2) % blocks
    return jnp.where((block_of(source) == one_side) | (block_of(source) == far), factor * array, array)


def block_scale(key, extent, cuts, smallest, top_value):
    def one(axis_at, blocks):
        draws = jax.random.uniform(jax.random.fold_in(jax.random.fold_in(key, 6), axis_at), (blocks,), jnp.float32, smallest / len(cuts), top_value / len(cuts))
        return jnp.repeat(jnp.exp(draws), extent[axis_at] // blocks).reshape((-1,) + (1,) * (len(extent) - axis_at - 1))

    factor_of = one(*cuts[0])
    for cut in cuts[1:]:
        factor_of = factor_of * one(*cut)
    return factor_of


def bell_draw(rng, dims, width, limit, shards=(), held_as=jnp.bfloat16):
    values = width * jax.random.normal(rng, dims, jnp.float32)
    if shards:
        values = values * block_scale(rng, dims, shards, -0.22, 0.18)
    return jnp.clip(values, -limit, limit).astype(held_as)


def bell_draw_with(own_key, extent, scale, bound, shards, heavy, kind=jnp.bfloat16):
    entries = scale * jax.random.normal(own_key, extent, jnp.float32)
    if shards:
        entries = entries * block_scale(own_key, extent, shards, -0.22, 0.18)
    return jnp.clip(spiked(entries, jax.random.fold_in(own_key, 3), *heavy), -bound, bound).astype(kind)


def setup_inputs(seed: int = 0, part: int = 0) -> dict:
    key_of = jax.random.split(jax.random.key(seed), 5)
    own_keys = jax.random.split(jax.random.fold_in(key_of[4], part), 5)
    return {
        "hidden": bell_draw(own_keys[0], (SECTIONS, ROWS, FF), 1.0, 6.0, ((0, 2), (2, 8))),
        "down_weight": bell_draw_with(key_of[1], (SECTIONS, FF, D), FF ** -0.5, 0.046875, ((0, 2), (1, 8)), (1, 2, 8, 2.0)),
        "stream": draw_stream(jax.random.fold_in(jax.random.fold_in(key_of[4], part), 71), part),
        "norm_gain": jnp.clip(1.0 + 0.15 * jax.random.normal(key_of[3], (SECTIONS, D), jnp.float32), 0.25, 1.75).astype(jnp.bfloat16),
    }


def reference(hidden, down_weight, stream, norm_gain):
    new_rows = []
    normed_rows = []
    for section_index in range(SECTIONS):
        projected = jnp.dot(hidden[section_index], down_weight[section_index], preferred_element_type=jnp.float32)
        updated = stream[section_index].astype(jnp.float32) + projected
        inverse = lax.rsqrt(lax.optimization_barrier(jnp.mean(updated * updated, axis=1, keepdims=True)) + 1e-05)
        normed = (updated * inverse * norm_gain[section_index].astype(jnp.float32)[None, :]).astype(jnp.bfloat16)
        new_rows.append(updated.astype(jnp.bfloat16))
        normed_rows.append(normed)
    new_stream = jnp.stack(new_rows, axis=0)
    next_input = jnp.roll(jnp.stack(normed_rows, axis=0), 1, axis=0)
    return (new_stream, next_input)
```

```python
import jax
import jax.numpy as jnp
from jax import lax
from jax.experimental import pallas as pl
from jax.experimental.pallas import tpu as pltpu
from jax.sharding import PartitionSpec as P

F32 = jnp.float32
WIRE = jnp.float16
TILE = 512


def matmul_kernel(order_ref, hidden_ref, weight_ref, out_ref):
    out_ref[0] = jnp.dot(hidden_ref[...], weight_ref[...], preferred_element_type=F32)


def chunk_products(hidden, weight, order, width):
    rows, depth = hidden.shape
    chunks = order.shape[0]
    tile = min(TILE, width)
    tiles = width // tile
    return pl.pallas_call(
        matmul_kernel,
        out_shape=jax.ShapeDtypeStruct((chunks, rows, width), F32),
        grid_spec=pltpu.PrefetchScalarGridSpec(
            num_scalar_prefetch=1,
            grid=(chunks, tiles),
            in_specs=[
                pl.BlockSpec((rows, depth), lambda c, j, order: (0, 0)),
                pl.BlockSpec((depth, tile), lambda c, j, order: (0, order[c] * tiles + j)),
            ],
            out_specs=pl.BlockSpec((1, rows, tile), lambda c, j, order: (c, 0, j)),
        ),
        compiler_params=pltpu.CompilerParams(vmem_limit_bytes=32 * 2**20),
        cost_estimate=pl.CostEstimate(
            flops=2 * rows * depth * width * chunks,
            bytes_accessed=2 * depth * width * chunks + 4 * rows * width * chunks,
            transcendentals=0,
        ),
        name="chunk_products",
    )(order, hidden, weight)


def send(block, pairs):
    return lax.ppermute(block, "tensor", pairs)


def reduce_line_of_four(hidden, weight, width):
    me = lax.axis_index("tensor")
    z, y = me // 2, me % 2
    upper = z >= 2
    outer = (z == 0) | (z == 3)
    toward = jnp.where(outer, jnp.array([3, 2, 1, 0]), jnp.array([3, 2, 0, 1]))
    places = jnp.where(upper, 3 - toward, toward)
    theirs = (2 * places + 1 - y).astype(jnp.int32)
    mine = (2 * places + y).astype(jnp.int32)

    across = [(t, t ^ 1) for t in range(8)]
    inward = [(0, 2), (1, 3), (6, 4), (7, 5)]
    middle = [(2, 4), (3, 5), (4, 2), (5, 3)]
    ends = [(t, t ^ 2) for t in range(8)]

    first = chunk_products(hidden, weight, theirs[:1], width)
    got = [send(first[0].astype(WIRE), across)]
    rest = chunk_products(hidden, weight, theirs[1:], width)
    got += [send(rest[i].astype(WIRE), across) for i in range(3)]
    own = chunk_products(hidden, weight, mine, width)

    def held(slot):
        return own[slot] + got[slot].astype(F32)

    sums = held(0)
    in_a = send(sums.astype(WIRE), inward)
    mid_a = send((sums + in_a.astype(F32)).astype(WIRE), middle)
    sums = held(1)
    in_b = send(sums.astype(WIRE), inward)
    mid_b = send((sums + in_b.astype(F32)).astype(WIRE), middle)
    last = send((held(2) + mid_a.astype(F32)).astype(WIRE), ends)
    return held(3) + last.astype(F32) + mid_b.astype(F32)


def per_device(hidden, down_weight, stream, norm_gain):
    count = lax.axis_size("tensor")
    full_width = down_weight.shape[2]
    width = full_width // count
    if count == 8:
        projected = reduce_line_of_four(hidden[0], down_weight[0], width)
    else:
        projected = lax.psum_scatter(
            jnp.dot(hidden[0], down_weight[0], preferred_element_type=F32),
            "tensor",
            scatter_dimension=1,
            tiled=True,
        )
    updated = stream[0].astype(F32) + projected
    swap = [(0, 1), (1, 0)]
    passed = lax.ppermute(updated * norm_gain[0].astype(F32)[None, :], "section", swap)
    squares = lax.ppermute(jnp.sum(updated * updated, axis=1), "section", swap)
    step = 1
    while step < count:
        squares = squares + send(squares, [(t, t ^ step) for t in range(count)])
        step *= 2
    inverse = lax.rsqrt(squares / full_width + 1e-05)
    normed = (passed * inverse[:, None]).astype(jnp.bfloat16)
    return (updated.astype(jnp.bfloat16)[None], normed[None])


def solution(mesh):
    in_specs = (
        P("section", "groups", "tensor"),
        P("section", "tensor", None),
        P("section", "groups", "tensor"),
        P("section", "tensor"),
    )
    out_specs = (P("section", "groups", "tensor"), P("section", "groups", "tensor"))
    return jax.shard_map(
        per_device, mesh=mesh, in_specs=in_specs, out_specs=out_specs, check_vma=False
    )
```

```python
import jax
import jax.numpy as jnp
from jax import lax
from jax.experimental import pallas as pl
from jax.experimental.pallas import tpu as pltpu
from jax.sharding import PartitionSpec as P

F32 = jnp.float32
WIRE = jnp.float16
TILE = 512


def matmul_kernel(order_ref, hidden_ref, weight_ref, out_ref):
    out_ref[0] = jnp.dot(hidden_ref[...], weight_ref[...], preferred_element_type=F32)


def chunk_products(hidden, weight, order, width):
    rows, depth = hidden.shape
    chunks = order.shape[0]
    tile = min(TILE, width)
    tiles = width // tile
    return pl.pallas_call(
        matmul_kernel,
        out_shape=jax.ShapeDtypeStruct((chunks, rows, width), F32),
        grid_spec=pltpu.PrefetchScalarGridSpec(
            num_scalar_prefetch=1,
            grid=(chunks, tiles),
            in_specs=[
                pl.BlockSpec((rows, depth), lambda c, j, order: (0, 0)),
                pl.BlockSpec((depth, tile), lambda c, j, order: (0, order[c] * tiles + j)),
            ],
            out_specs=pl.BlockSpec((1, rows, tile), lambda c, j, order: (c, 0, j)),
        ),
        compiler_params=pltpu.CompilerParams(vmem_limit_bytes=32 * 2**20),
        cost_estimate=pl.CostEstimate(
            flops=2 * rows * depth * width * chunks,
            bytes_accessed=2 * depth * width * chunks + 4 * rows * width * chunks,
            transcendentals=0,
        ),
        name="chunk_products",
    )(order, hidden, weight)


def send(block, pairs):
    return lax.ppermute(block, "tensor", pairs)


def reduce_line_of_four(hidden, weight, width):
    me = lax.axis_index("tensor")
    z, y = me // 2, me % 2
    upper = z >= 2
    outer = (z == 0) | (z == 3)
    toward = jnp.where(outer, jnp.array([3, 2, 1, 0]), jnp.array([3, 2, 0, 1]))
    places = jnp.where(upper, 3 - toward, toward)
    theirs = (2 * places + 1 - y).astype(jnp.int32)
    mine = (2 * places + y).astype(jnp.int32)

    across = [(t, t ^ 1) for t in range(8)]
    inward = [(0, 2), (1, 3), (6, 4), (7, 5)]
    middle = [(2, 4), (3, 5), (4, 2), (5, 3)]
    ends = [(t, t ^ 2) for t in range(8)]

    def both(indices):
        return chunk_products(hidden, weight, jnp.concatenate(indices), width)

    def cross(block):
        return send(block.astype(WIRE), across)

    first = chunk_products(hidden, weight, theirs[:1], width)
    got = [cross(first[0])]
    second = both((theirs[1:2], mine[:1]))
    got.append(cross(second[0]))
    third = both((theirs[2:3], mine[1:2]))
    got.append(cross(third[0]))
    fourth = both((theirs[3:], mine[2:]))
    got.append(cross(fourth[0]))
    own = [second[1], third[1], fourth[1], fourth[2]]

    def held(slot):
        return own[slot] + got[slot].astype(F32)

    sums = held(0)
    in_a = send(sums.astype(WIRE), inward)
    mid_a = send((sums + in_a.astype(F32)).astype(WIRE), middle)
    sums = held(1)
    in_b = send(sums.astype(WIRE), inward)
    mid_b = send((sums + in_b.astype(F32)).astype(WIRE), middle)
    last = send((held(2) + mid_a.astype(F32)).astype(WIRE), ends)
    return held(3) + last.astype(F32) + mid_b.astype(F32)


def total_squares(squares, count):
    swap = [(0, 1), (1, 0)]
    if count != 8:
        squares = lax.ppermute(squares, "section", swap)
        step = 1
        while step < count:
            squares = squares + send(squares, [(t, t ^ step) for t in range(count)])
            step *= 2
        return squares
    corner = [(2 * t + s, 2 * (t ^ 1) + 1 - s) for t in range(8) for s in range(2)]
    squares = lax.ppermute(squares, "section", swap) + lax.ppermute(
        squares, ("tensor", "section"), corner
    )
    others = [send(squares, [(t, t ^ step) for t in range(8)]) for step in (2, 4, 6)]
    return squares + others[0] + (others[1] + others[2])


def per_device(hidden, down_weight, stream, norm_gain):
    count = lax.axis_size("tensor")
    full_width = down_weight.shape[2]
    width = full_width // count
    if count == 8:
        projected = reduce_line_of_four(hidden[0], down_weight[0], width)
    else:
        projected = lax.psum_scatter(
            jnp.dot(hidden[0], down_weight[0], preferred_element_type=F32),
            "tensor",
            scatter_dimension=1,
            tiled=True,
        )
    updated = stream[0].astype(F32) + projected
    squares = total_squares(jnp.sum(updated * updated, axis=1), count)
    scaled = updated * norm_gain[0].astype(F32)[None, :]
    passed = lax.ppermute(scaled, "section", [(0, 1), (1, 0)])
    inverse = lax.rsqrt(squares / full_width + 1e-05)
    normed = (passed * inverse[:, None]).astype(jnp.bfloat16)
    return (updated.astype(jnp.bfloat16)[None], normed[None])


def solution(mesh):
    in_specs = (
        P("section", "groups", "tensor"),
        P("section", "tensor", None),
        P("section", "groups", "tensor"),
        P("section", "tensor"),
    )
    out_specs = (P("section", "groups", "tensor"), P("section", "groups", "tensor"))
    return jax.shard_map(
        per_device, mesh=mesh, in_specs=in_specs, out_specs=out_specs, check_vma=False
    )
```

```python
import jax
import jax.numpy as jnp
from jax import lax
from jax.experimental import pallas as pl
from jax.experimental.pallas import tpu as pltpu
from jax.sharding import PartitionSpec as P

F32 = jnp.float32
WIRE = jnp.float16


def tile_products(hidden, weight, place, order, tile):
    rows, depth = hidden.shape
    counts = [len(tiles) for tiles in order]
    starts = [sum(counts[:i]) for i in range(len(counts))]
    listed = [tile for tiles in order for tile in tiles]

    def kernel(place_ref, hidden_ref, weight_ref, *out_refs):
        step = pl.program_id(0)
        for out_ref, start, count in zip(out_refs, starts, counts):

            @pl.when((step >= start) & (step < start + count))
            def _(out_ref=out_ref):
                out_ref[...] = jnp.dot(
                    hidden_ref[...], weight_ref[...], preferred_element_type=F32
                )

    def weight_tile(j, place):
        z, y = place[0] // 2, place[0] % 2
        slots = (3 - 3 * (z // 2), 2 - z // 2, z + 1 - 2 * (z % 2), z)
        places = [4 * slots[s] + 2 * (1 - y if other else y) + half for other, s, half in listed]
        column = places[0]
        for i in range(1, len(places)):
            column = jnp.where(j >= i, places[i], column)
        return (0, column)

    def out_tile(start, count):
        return lambda j, place: (0, jnp.clip(j - start, 0, count - 1))

    return pl.pallas_call(
        kernel,
        out_shape=[jax.ShapeDtypeStruct((rows, n * tile), F32) for n in counts],
        grid_spec=pltpu.PrefetchScalarGridSpec(
            num_scalar_prefetch=1,
            grid=(len(listed),),
            in_specs=[
                pl.BlockSpec((rows, depth), lambda j, place: (0, 0)),
                pl.BlockSpec((depth, tile), weight_tile),
            ],
            out_specs=[
                pl.BlockSpec((rows, tile), out_tile(s, n)) for s, n in zip(starts, counts)
            ],
        ),
        compiler_params=pltpu.CompilerParams(vmem_limit_bytes=32 * 2**20),
        cost_estimate=pl.CostEstimate(
            flops=2 * rows * depth * tile * len(listed),
            bytes_accessed=(2 * depth + 4 * rows) * tile * len(listed),
            transcendentals=0,
        ),
        name="tile_products",
    )(place, hidden, weight)


def send(block, pairs):
    return lax.ppermute(block, "tensor", pairs)


def after(array, *earlier):
    return lax.optimization_barrier((array, *earlier))[0]


def reduce_line_of_four(hidden, weight, width):
    place = lax.axis_index("tensor").astype(jnp.int32)[None]
    tile = width // 2

    across = [(t, t ^ 1) for t in range(8)]
    inward = [(0, 2), (1, 3), (6, 4), (7, 5)]
    middle = [(2, 4), (3, 5), (4, 2), (5, 3)]
    ends = [(t, t ^ 2) for t in range(8)]
    beyond = [(2, 6), (3, 7), (4, 0), (5, 1)]

    def products(order, *earlier):
        here = after(place, *earlier) if earlier else place
        return tile_products(hidden, weight, here, order, tile)

    def theirs(slot, *halves):
        return [(1, slot, half) for half in halves or (0, 1)]

    def mine(slot, *halves):
        return [(0, slot, half) for half in halves or (0, 1)]

    def narrow(block):
        return block.astype(WIRE)

    def wide(block):
        return block.astype(F32)

    def join(left, right):
        return jnp.concatenate([left, right], axis=1)

    [first] = products([theirs(0, 0)])
    first = narrow(first)
    y0a = send(first, across)
    second, own0a = products([theirs(0, 1), mine(0, 0)], first)
    second = narrow(second)
    y0b = send(second, across)
    third, own0b = products([theirs(1), mine(0, 1)], second, y0a)
    third = narrow(third)
    y1 = send(third, across)
    sum0 = join(own0a + wide(y0a), own0b + wide(after(y0b, third)))
    out0 = narrow(sum0)
    in0 = send(out0, inward)
    fourth, own1 = products([theirs(2), mine(1)], third, out0)
    fourth = narrow(fourth)
    y2 = send(fourth, across)
    sum1 = own1 + wide(after(y1, own1))
    out1 = narrow(sum1)
    in1 = send(out1, inward)
    passed0 = narrow(sum0 + wide(after(in0, out1)))
    far0 = send(passed0, beyond)
    fifth, own2 = products([theirs(3), mine(2)], fourth, out1, passed0)
    fifth = narrow(fifth)
    y3 = send(fifth, across)
    passed1 = narrow(sum1 + wide(after(in1, own2)))
    mid1 = send(passed1, middle)
    out2 = narrow(own2 + wide(after(y2, own2)))
    last = send(out2, ends)
    [own3] = products([mine(3)], fifth, out2, passed1)
    return own3 + wide(y3) + wide(last) + wide(far0) + wide(mid1)


def total_squares(squares, count):
    swap = [(0, 1), (1, 0)]
    if count != 8:
        squares = lax.ppermute(squares, "section", swap)
        step = 1
        while step < count:
            squares = squares + send(squares, [(t, t ^ step) for t in range(count)])
            step *= 2
        return squares
    corner = [(2 * t + s, 2 * (t ^ 1) + 1 - s) for t in range(8) for s in range(2)]
    squares = lax.ppermute(squares, "section", swap) + lax.ppermute(
        squares, ("tensor", "section"), corner
    )
    others = [send(squares, [(t, t ^ step) for t in range(8)]) for step in (2, 4, 6)]
    return squares + others[0] + (others[1] + others[2])


def per_device(hidden, down_weight, stream, norm_gain):
    count = lax.axis_size("tensor")
    full_width = down_weight.shape[2]
    width = full_width // count
    if count == 8:
        projected = reduce_line_of_four(hidden[0], down_weight[0], width)
    else:
        projected = lax.psum_scatter(
            jnp.dot(hidden[0], down_weight[0], preferred_element_type=F32),
            "tensor",
            scatter_dimension=1,
            tiled=True,
        )
    updated = stream[0].astype(F32) + projected
    squares = total_squares(jnp.sum(updated * updated, axis=1), count)
    scaled = updated * norm_gain[0].astype(F32)[None, :]
    passed = lax.ppermute(scaled, "section", [(0, 1), (1, 0)])
    inverse = lax.rsqrt(squares / full_width + 1e-05)
    normed = (passed * inverse[:, None]).astype(jnp.bfloat16)
    return (updated.astype(jnp.bfloat16)[None], normed[None])


def solution(mesh):
    in_specs = (
        P("section", "groups", "tensor"),
        P("section", "tensor", None),
        P("section", "groups", "tensor"),
        P("section", "tensor"),
    )
    out_specs = (P("section", "groups", "tensor"), P("section", "groups", "tensor"))
    return jax.shard_map(
        per_device, mesh=mesh, in_specs=in_specs, out_specs=out_specs, check_vma=False
    )
```

```python
import jax
import jax.numpy as jnp
from jax import lax
from jax.experimental import pallas as pl
from jax.experimental.pallas import tpu as pltpu
from jax.sharding import PartitionSpec as P

F32 = jnp.float32
WIRE = jnp.float16


def tile_products(hidden, weight, place, order, tile):
    rows, depth = hidden.shape
    counts = [len(tiles) for tiles in order]
    starts = [sum(counts[:i]) for i in range(len(counts))]
    listed = [tile for tiles in order for tile in tiles]

    def kernel(place_ref, hidden_ref, weight_ref, *out_refs):
        step = pl.program_id(0)
        for out_ref, start, count in zip(out_refs, starts, counts):

            @pl.when((step >= start) & (step < start + count))
            def _(out_ref=out_ref):
                out_ref[...] = jnp.dot(
                    hidden_ref[...], weight_ref[...], preferred_element_type=F32
                )

    def weight_tile(j, place):
        z, y = place[0] // 2, place[0] % 2
        slots = (3 - 3 * (z // 2), 2 - z // 2, z + 1 - 2 * (z % 2), z)
        places = [4 * slots[s] + 2 * (1 - y if other else y) + half for other, s, half in listed]
        column = places[0]
        for i in range(1, len(places)):
            column = jnp.where(j >= i, places[i], column)
        return (0, column)

    def out_tile(start, count):
        return lambda j, place: (0, jnp.clip(j - start, 0, count - 1))

    return pl.pallas_call(
        kernel,
        out_shape=[jax.ShapeDtypeStruct((rows, n * tile), F32) for n in counts],
        grid_spec=pltpu.PrefetchScalarGridSpec(
            num_scalar_prefetch=1,
            grid=(len(listed),),
            in_specs=[
                pl.BlockSpec((rows, depth), lambda j, place: (0, 0)),
                pl.BlockSpec((depth, tile), weight_tile),
            ],
            out_specs=[
                pl.BlockSpec((rows, tile), out_tile(s, n)) for s, n in zip(starts, counts)
            ],
        ),
        compiler_params=pltpu.CompilerParams(vmem_limit_bytes=32 * 2**20),
        cost_estimate=pl.CostEstimate(
            flops=2 * rows * depth * tile * len(listed),
            bytes_accessed=(2 * depth + 4 * rows) * tile * len(listed),
            transcendentals=0,
        ),
        name="tile_products",
    )(place, hidden, weight)


def send(block, pairs):
    return lax.ppermute(block, "tensor", pairs)


def after(array, *earlier):
    return lax.optimization_barrier((array, *earlier))[0]


def reduce_line_of_four(hidden, weight, width):
    place = lax.axis_index("tensor").astype(jnp.int32)[None]
    tile = width // 2

    across = [(t, t ^ 1) for t in range(8)]
    inward = [(0, 2), (1, 3), (6, 4), (7, 5)]
    middle = [(2, 4), (3, 5), (4, 2), (5, 3)]
    ends = [(t, t ^ 2) for t in range(8)]
    beyond = [(2, 6), (3, 7), (4, 0), (5, 1)]

    def products(order, *earlier):
        here = after(place, *earlier) if earlier else place
        return tile_products(hidden, weight, here, order, tile)

    def theirs(slot, *halves):
        return [(1, slot, half) for half in halves or (0, 1)]

    def mine(slot, *halves):
        return [(0, slot, half) for half in halves or (0, 1)]

    def narrow(block):
        return block.astype(WIRE)

    def wide(block):
        return block.astype(F32)

    def join(left, right):
        return jnp.concatenate([left, right], axis=1)

    me = lax.axis_index("tensor")
    column = 4 * (3 - 3 * (me // 4)) + 2 * (1 - me % 2)
    first = jnp.dot(
        hidden,
        lax.dynamic_slice_in_dim(weight, column * tile, tile, 1),
        preferred_element_type=F32,
    )
    first = narrow(first)
    y0a = send(first, across)
    second, own0a = products([theirs(0, 1), mine(0, 0)], first)
    second = narrow(second)
    y0b = send(second, across)
    third, own0b = products([theirs(1), mine(0, 1)], second, y0a)
    third = narrow(third)
    y1 = send(third, across)
    sum0 = join(own0a, own0b) + wide(join(y0a, after(y0b, own0b)))
    out0 = narrow(sum0)
    in0 = send(out0, inward)
    fourth, own1 = products([theirs(2), mine(1)], third, out0)
    fourth = narrow(fourth)
    y2 = send(fourth, across)
    sum1 = own1 + wide(after(y1, own1))
    out1 = narrow(sum1)
    in1 = send(out1, inward)
    passed0 = narrow(sum0 + wide(after(in0, out1)))
    far0 = send(passed0, beyond)
    fifth, own2 = products([theirs(3), mine(2)], fourth, out1, passed0)
    fifth = narrow(fifth)
    y3 = send(fifth, across)
    passed1 = narrow(sum1 + wide(after(in1, fifth)))
    mid1 = send(passed1, middle)
    out2 = narrow(own2 + wide(after(y2, passed1)))
    last = send(out2, ends)
    [own3] = products([mine(3)], fifth, out2, passed1)
    return own3 + wide(y3) + wide(last) + wide(far0) + wide(mid1)


def swapped(block):
    return lax.ppermute(block, "section", [(0, 1), (1, 0)])


def first_round(squares, count):
    if count == 1:
        return swapped(squares)
    corner = [(2 * t + s, 2 * (t ^ 1) + 1 - s) for t in range(count) for s in range(2)]
    return swapped(squares) + lax.ppermute(squares, ("tensor", "section"), corner)


def other_rounds(squares, count):
    if count == 8:
        near, far, beyond = [send(squares, [(t, t ^ step) for t in range(8)]) for step in (2, 4, 6)]
        return squares + near + (far + beyond)
    step = 2
    while step < count:
        squares = squares + send(squares, [(t, t ^ step) for t in range(count)])
        step *= 2
    return squares


def per_device(hidden, down_weight, stream, norm_gain):
    count = lax.axis_size("tensor")
    full_width = down_weight.shape[2]
    width = full_width // count
    if count == 8:
        projected = reduce_line_of_four(hidden[0], down_weight[0], width)
    else:
        projected = lax.psum_scatter(
            jnp.dot(hidden[0], down_weight[0], preferred_element_type=F32),
            "tensor",
            scatter_dimension=1,
            tiled=True,
        )
    updated = stream[0].astype(F32) + projected
    squares = first_round(jnp.sum(updated * updated, axis=1), count)
    gain = norm_gain[0].astype(F32)
    passed = swapped(after(updated, squares) * gain[None, :])
    squares = other_rounds(squares, count)
    inverse = lax.rsqrt(squares / full_width + 1e-05)
    normed = (passed * inverse[:, None]).astype(jnp.bfloat16)
    return (updated.astype(jnp.bfloat16)[None], normed[None])


def solution(mesh):
    in_specs = (
        P("section", "groups", "tensor"),
        P("section", "tensor", None),
        P("section", "groups", "tensor"),
        P("section", "tensor"),
    )
    out_specs = (P("section", "groups", "tensor"), P("section", "groups", "tensor"))
    return jax.shard_map(
        per_device, mesh=mesh, in_specs=in_specs, out_specs=out_specs, check_vma=False
    )
```

```python
import jax
import jax.numpy as jnp
from jax import lax
from jax.experimental import pallas as pl
from jax.experimental.pallas import tpu as pltpu
from jax.sharding import PartitionSpec as P

F32 = jnp.float32
WIRE = jnp.float16


def tile_products(hidden, weight, place, order, tile):
    rows, depth = hidden.shape
    counts = [len(tiles) for tiles in order]
    starts = [sum(counts[:i]) for i in range(len(counts))]
    listed = [tile for tiles in order for tile in tiles]

    def kernel(place_ref, hidden_ref, weight_ref, *out_refs):
        step = pl.program_id(0)
        for out_ref, start, count in zip(out_refs, starts, counts):

            @pl.when((step >= start) & (step < start + count))
            def _(out_ref=out_ref):
                out_ref[...] = jnp.dot(
                    hidden_ref[...], weight_ref[...], preferred_element_type=F32
                )

    def weight_tile(j, place):
        z, y = place[0] // 2, place[0] % 2
        slots = (3 - 3 * (z // 2), 2 - z // 2, z + 1 - 2 * (z % 2), z)
        places = [4 * slots[s] + 2 * (1 - y if other else y) + half for other, s, half in listed]
        column = places[0]
        for i in range(1, len(places)):
            column = jnp.where(j >= i, places[i], column)
        return (0, column)

    def out_tile(start, count):
        return lambda j, place: (0, jnp.clip(j - start, 0, count - 1))

    return pl.pallas_call(
        kernel,
        out_shape=[jax.ShapeDtypeStruct((rows, n * tile), F32) for n in counts],
        grid_spec=pltpu.PrefetchScalarGridSpec(
            num_scalar_prefetch=1,
            grid=(len(listed),),
            in_specs=[
                pl.BlockSpec((rows, depth), lambda j, place: (0, 0)),
                pl.BlockSpec((depth, tile), weight_tile),
            ],
            out_specs=[
                pl.BlockSpec((rows, tile), out_tile(s, n)) for s, n in zip(starts, counts)
            ],
        ),
        compiler_params=pltpu.CompilerParams(vmem_limit_bytes=24 * 2**20),
        cost_estimate=pl.CostEstimate(
            flops=2 * rows * depth * tile * len(listed),
            bytes_accessed=(2 * depth + 4 * rows) * tile * len(listed),
            transcendentals=0,
        ),
        name="tile_products",
    )(place, hidden, weight)


def send(block, pairs):
    return lax.ppermute(block, "tensor", pairs)


def after(array, *earlier):
    return lax.optimization_barrier((array, *earlier))[0]


def reduce_line_of_four(hidden, weight, width):
    place = lax.axis_index("tensor").astype(jnp.int32)[None]
    tile = width // 2

    across = [(t, t ^ 1) for t in range(8)]
    inward = [(0, 2), (1, 3), (6, 4), (7, 5)]
    middle = [(2, 4), (3, 5), (4, 2), (5, 3)]
    ends = [(t, t ^ 2) for t in range(8)]
    beyond = [(2, 6), (3, 7), (4, 0), (5, 1)]

    def products(order, *earlier):
        here = after(place, *earlier) if earlier else place
        return tile_products(hidden, weight, here, order, tile)

    def theirs(slot, *halves):
        return [(1, slot, half) for half in halves or (0, 1)]

    def mine(slot, *halves):
        return [(0, slot, half) for half in halves or (0, 1)]

    def narrow(block):
        return block.astype(WIRE)

    def wide(block):
        return block.astype(F32)

    def join(left, right):
        return jnp.concatenate([left, right], axis=1)

    me = lax.axis_index("tensor")
    column = 4 * (3 - 3 * (me // 4)) + 2 * (1 - me % 2)
    first = jnp.dot(
        hidden,
        lax.dynamic_slice_in_dim(weight, column * tile, tile, 1),
        preferred_element_type=F32,
    )
    first = narrow(first)
    y0a = send(first, across)
    second, own0a = products([theirs(0, 1), mine(0, 0)], first)
    second = narrow(second)
    y0b = send(second, across)
    third, own0b = products([theirs(1), mine(0, 1)], second, y0a)
    third = narrow(third)
    y1 = send(third, across)
    sum0 = join(own0a, own0b) + wide(join(y0a, after(y0b, own0b)))
    out0 = narrow(sum0)
    in0 = send(out0, inward)
    fourth, own1 = products([theirs(2), mine(1)], third, out0)
    fourth = narrow(fourth)
    y2 = send(fourth, across)
    sum1 = own1 + wide(after(y1, own1))
    out1 = narrow(sum1)
    in1 = send(out1, inward)
    passed0 = narrow(sum0 + wide(after(in0, out1)))
    far0 = send(passed0, beyond)
    fifth, own2 = products([theirs(3), mine(2)], fourth, out1, passed0)
    fifth = narrow(fifth)
    y3 = send(fifth, across)
    passed1 = narrow(sum1 + wide(after(in1, fifth)))
    mid1 = send(passed1, middle)
    out2 = narrow(own2 + wide(after(y2, passed1)))
    last = send(out2, ends)
    [own3] = products([mine(3)], fifth, out2, passed1)
    return own3 + wide(y3) + wide(last) + wide(far0) + wide(mid1)


def swapped(block):
    return lax.ppermute(block, "section", [(0, 1), (1, 0)])


def first_round(squares, count):
    if count == 1:
        return swapped(squares)
    corner = [(2 * t + s, 2 * (t ^ 1) + 1 - s) for t in range(count) for s in range(2)]
    return swapped(squares) + lax.ppermute(squares, ("tensor", "section"), corner)


def other_rounds(squares, count):
    if count == 8:
        near, far, beyond = [send(squares, [(t, t ^ step) for t in range(8)]) for step in (2, 4, 6)]
        return squares + near + (far + beyond)
    step = 2
    while step < count:
        squares = squares + send(squares, [(t, t ^ step) for t in range(count)])
        step *= 2
    return squares


def per_device(hidden, down_weight, stream, norm_gain):
    count = lax.axis_size("tensor")
    full_width = down_weight.shape[2]
    width = full_width // count
    if count == 8:
        projected = reduce_line_of_four(hidden[0], down_weight[0], width)
    else:
        projected = lax.psum_scatter(
            jnp.dot(hidden[0], down_weight[0], preferred_element_type=F32),
            "tensor",
            scatter_dimension=1,
            tiled=True,
        )
    updated = stream[0].astype(F32) + projected
    squares = first_round(jnp.sum(updated * updated, axis=1), count)
    gain = norm_gain[0].astype(F32)
    passed = swapped(after(updated, squares) * gain[None, :])
    squares = other_rounds(squares, count)
    inverse = lax.rsqrt(squares / full_width + 1e-05)
    normed = (passed * inverse[:, None]).astype(jnp.bfloat16)
    return (updated.astype(jnp.bfloat16)[None], normed[None])


def solution(mesh):
    in_specs = (
        P("section", "groups", "tensor"),
        P("section", "tensor", None),
        P("section", "groups", "tensor"),
        P("section", "tensor"),
    )
    out_specs = (P("section", "groups", "tensor"), P("section", "groups", "tensor"))
    return jax.shard_map(
        per_device, mesh=mesh, in_specs=in_specs, out_specs=out_specs, check_vma=False
    )
```

```python
import jax
import jax.numpy as jnp
from jax import lax
from jax.experimental import pallas as pl
from jax.experimental.pallas import tpu as pltpu
from jax.sharding import PartitionSpec as P

F32 = jnp.float32
WIRE = jnp.float16


def tile_products(hidden, weight, place, order, tile):
    rows, depth = hidden.shape
    counts = [len(tiles) for tiles in order]
    starts = [sum(counts[:i]) for i in range(len(counts))]
    listed = [tile for tiles in order for tile in tiles]

    def kernel(place_ref, hidden_ref, weight_ref, *out_refs):
        step = pl.program_id(0)
        for out_ref, start, count in zip(out_refs, starts, counts):

            @pl.when((step >= start) & (step < start + count))
            def _(out_ref=out_ref):
                out_ref[...] = jnp.dot(
                    hidden_ref[...], weight_ref[...], preferred_element_type=F32
                )

    def weight_tile(j, place):
        z, y = place[0] // 2, place[0] % 2
        slots = (3 - 3 * (z // 2), 2 - z // 2, z + 1 - 2 * (z % 2), z)
        places = [4 * slots[s] + 2 * (1 - y if other else y) + half for other, s, half in listed]
        column = places[0]
        for i in range(1, len(places)):
            column = jnp.where(j >= i, places[i], column)
        return (0, column)

    def out_tile(start, count):
        return lambda j, place: (0, jnp.clip(j - start, 0, count - 1))

    return pl.pallas_call(
        kernel,
        out_shape=[jax.ShapeDtypeStruct((rows, n * tile), F32) for n in counts],
        grid_spec=pltpu.PrefetchScalarGridSpec(
            num_scalar_prefetch=1,
            grid=(len(listed),),
            in_specs=[
                pl.BlockSpec((rows, depth), lambda j, place: (0, 0)),
                pl.BlockSpec((depth, tile), weight_tile),
            ],
            out_specs=[
                pl.BlockSpec((rows, tile), out_tile(s, n)) for s, n in zip(starts, counts)
            ],
        ),
        compiler_params=pltpu.CompilerParams(vmem_limit_bytes=24 * 2**20),
        cost_estimate=pl.CostEstimate(
            flops=2 * rows * depth * tile * len(listed),
            bytes_accessed=(2 * depth + 4 * rows) * tile * len(listed),
            transcendentals=0,
        ),
        name="tile_products",
    )(place, hidden, weight)


def send(block, pairs):
    return lax.ppermute(block, "tensor", pairs)


def after(array, *earlier):
    return lax.optimization_barrier((array, *earlier))[0]


def reduce_line_of_four(hidden, weight, width):
    place = lax.axis_index("tensor").astype(jnp.int32)[None]
    tile = width // 2

    across = [(t, t ^ 1) for t in range(8)]
    inward = [(0, 2), (1, 3), (6, 4), (7, 5)]
    middle = [(2, 4), (3, 5), (4, 2), (5, 3)]
    ends = [(t, t ^ 2) for t in range(8)]
    beyond = [(2, 6), (3, 7), (4, 0), (5, 1)]

    def products(order, *earlier):
        here = after(place, *earlier) if earlier else place
        return tile_products(hidden, weight, here, order, tile)

    def theirs(slot, *halves):
        return [(1, slot, half) for half in halves or (0, 1)]

    def mine(slot, *halves):
        return [(0, slot, half) for half in halves or (0, 1)]

    def narrow(block):
        return block.astype(WIRE)

    def wide(block):
        return block.astype(F32)

    def join(left, right):
        return jnp.concatenate([left, right], axis=1)

    me = lax.axis_index("tensor")
    column = 4 * (3 - 3 * (me // 4)) + 2 * (1 - me % 2)
    first = jnp.dot(
        hidden,
        lax.dynamic_slice_in_dim(weight, column * tile, tile, 1),
        preferred_element_type=F32,
    )
    first = narrow(first)
    y0a = send(first, across)
    second, own0a = products([theirs(0, 1), mine(0, 0)], first)
    second = narrow(second)
    y0b = send(second, across)
    third, own0b = products([theirs(1), mine(0, 1)], second, y0a)
    third = narrow(third)
    y1 = send(third, across)
    sum0 = join(own0a, own0b) + wide(join(y0a, after(y0b, own0b)))
    out0 = narrow(sum0)
    in0 = send(out0, inward)
    fourth, own1 = products([theirs(2), mine(1)], third, out0)
    fourth = narrow(fourth)
    y2 = send(fourth, across)
    sum1 = own1 + wide(after(y1, own1))
    out1 = narrow(sum1)
    in1 = send(out1, inward)
    passed0 = narrow(sum0 + wide(after(in0, out1)))
    far0 = send(passed0, beyond)
    fifth, own2 = products([theirs(3), mine(2)], fourth, out1, passed0)
    fifth = narrow(fifth)
    y3 = send(fifth, across)
    passed1 = narrow(sum1 + wide(after(in1, fifth)))
    mid1 = send(passed1, middle)
    out2 = narrow(own2 + wide(after(y2, passed1)))
    last = send(out2, ends)
    [own3] = products([mine(3)], fifth, out2, passed1)
    arrived = lax.optimization_barrier(own3 + wide(far0) + wide(y3))
    return arrived + wide(last) + wide(mid1)


def swapped(block):
    return lax.ppermute(block, "section", [(0, 1), (1, 0)])


def first_round(squares, count):
    if count == 1:
        return swapped(squares)
    corner = [(2 * t + s, 2 * (t ^ 1) + 1 - s) for t in range(count) for s in range(2)]
    return swapped(squares) + lax.ppermute(squares, ("tensor", "section"), corner)


def other_rounds(squares, count):
    if count == 8:
        near, far, beyond = [send(squares, [(t, t ^ step) for t in range(8)]) for step in (2, 4, 6)]
        return squares + near + (far + beyond)
    step = 2
    while step < count:
        squares = squares + send(squares, [(t, t ^ step) for t in range(count)])
        step *= 2
    return squares


def per_device(hidden, down_weight, stream, norm_gain):
    count = lax.axis_size("tensor")
    full_width = down_weight.shape[2]
    width = full_width // count
    if count == 8:
        projected = reduce_line_of_four(hidden[0], down_weight[0], width)
    else:
        projected = lax.psum_scatter(
            jnp.dot(hidden[0], down_weight[0], preferred_element_type=F32),
            "tensor",
            scatter_dimension=1,
            tiled=True,
        )
    updated = stream[0].astype(F32) + projected
    squares = first_round(jnp.sum(updated * updated, axis=1), count)
    gain = norm_gain[0].astype(F32)
    passed = swapped(after(updated, squares) * gain[None, :])
    squares = other_rounds(squares, count)
    inverse = lax.rsqrt(squares / full_width + 1e-05)
    normed = (passed * inverse[:, None]).astype(jnp.bfloat16)
    return (updated.astype(jnp.bfloat16)[None], normed[None])


def solution(mesh):
    in_specs = (
        P("section", "groups", "tensor"),
        P("section", "tensor", None),
        P("section", "groups", "tensor"),
        P("section", "tensor"),
    )
    out_specs = (P("section", "groups", "tensor"), P("section", "groups", "tensor"))
    return jax.shard_map(
        per_device, mesh=mesh, in_specs=in_specs, out_specs=out_specs, check_vma=False
    )
```
